128 devices in a mesh: sta: 16 (over x, z), tpl: 8 (over y, core).
Axes of the slice: x: 4, y: 4, z: 4, core: 2. Of those that a mesh axis runs over, the one named last changes fastest.
Arguments:
- records: bfloat16 [1024, 3, 4480], P(('sta', 'tpl')), may hold values from -6 to 6
- templates: bfloat16 [3072, 10, 3, 200], P(('sta', 'tpl')), may hold values from -6 to 6
- pick_owner: int32 [3072, 10], P(('sta', 'tpl')), may hold values from 0 to 127, all different within a row; in each aligned block of 24 rows (0 to 23, 24 to 47, ...) at most 3 rows name the same one
- pick_local: int32 [3072, 10], P(('sta', 'tpl')), may hold values from 0 to 7
- moveout: int32 [3072, 10], P(('sta', 'tpl')), may hold values from 0 to 127
- channel_mask: int32 [3072, 10, 3], P(('sta', 'tpl')), may hold values 0 or 1
Outputs:
- detection: float32 [3072, 4096], P(('sta', 'tpl'))
The draws below stay inside these ranges and needn't reach their ends.
Inputs may be any that keep to these rules, and one draw needn't show every extreme that they name: `pick_owner`: each template names 10 different devices; among the templates of one device no device is named more than 3 times, and some device is named exactly 3 times.
All inputs are finite; a program needn't handle non-finite values. No bound on the sum of `channel_mask` on one device may be relied on, other than what follows from the above.
Results may differ from the reference program's by a relative error of at most 0.0029.
Values may be sent and summed in bfloat16 or wider, within the bound.
No kernel may reach another device: no remote copies, remote signals or barrier semaphores. Data moves between devices by JAX's collectives and lax.ppermute only.
A program may use at most 128 MiB of HBM per device.

```python
import math
import jax
import jax.numpy as jnp
import numpy as np
from jax import lax

STA_LOC = 8
TPL_LOC = 24
LAGS = 4096
PICKS = 10
TLEN = 200
DLEN = 4480
CAP = 3
STATIONS = 1024
TEMPLATES = 3072
DEVICES = 128


def set_ends(values, rng, least, largest):
    longest = values.shape.index(max(values.shape))
    spots = []
    for shift in (0, 1):
        where = [jax.random.randint(jax.random.fold_in(rng, axis), (), 0, length) for axis, length in enumerate(values.shape)]
        where[longest] = (where[longest] + shift) % values.shape[longest]
        spots.append(tuple(where))
    return values.at[spots[0]].set(least).at[spots[1]].set(largest)


def level_of(own_key, dims, cuts, least, top_value):
    gain, own = 1.0, jax.random.fold_in(own_key, 6)
    for axis_at, blocks in cuts:
        steps = jnp.exp(jax.random.uniform(jax.random.fold_in(own, axis_at), (blocks,), jnp.float32, least / len(cuts), top_value / len(cuts)))
        gain = gain * jnp.repeat(steps, dims[axis_at] // blocks).reshape([-1 if axis == axis_at else 1 for axis in range(len(dims))])
    return gain


def routed_block(key, own, number, rows, count, top, limit, lean):
    order = jax.random.permutation(key, count)
    crowded, usual = load_shares(count, rows * top, limit, lean, True), load_shares(count, rows * top, limit, lean, False)
    places = jnp.arange(count)

    def named(tallies, offset_by):
        used = int((tallies > 0).sum())
        fixed = max(1, used // 4)
        shifted = fixed + (places - fixed + offset_by * (used - fixed)) % max(1, count - fixed)
        return jnp.zeros((count,), jnp.int32).at[order[jnp.where(places < fixed, places, shifted)]].set(jnp.asarray(tallies, jnp.int32))

    tallies = jnp.where(number % 4 == 0, named(crowded, number // 4), named(usual, number - number // 4 - 1))
    mixed = jax.random.permutation(jax.random.fold_in(own, 3), count)
    giver, sink = mixed[0:count // 2 * 2:2], mixed[1:count // 2 * 2:2]
    slack = jnp.minimum(tallies[giver] - 1, limit - tallies[sink]) // 2
    slack = jnp.where((giver == order[0]) | (sink == order[0]) | (tallies[sink] == 0), 0, jnp.maximum(slack, 0))
    shifted = jax.random.randint(jax.random.fold_in(own, 4), (count // 2,), 0, 1 << 20) % (slack + 1)
    tallies = tallies.at[giver].add(-shifted).at[sink].add(shifted)
    labels = jnp.searchsorted(jnp.cumsum(tallies), jnp.arange(rows * top), side="right").astype(jnp.int32)
    table = labels.reshape(top, rows).T
    table = table[jax.random.permutation(jax.random.fold_in(own, 1), rows)]
    offset_by = jax.random.randint(jax.random.fold_in(own, 2), (rows, 1), 0, top)
    return jnp.take_along_axis(table, (jnp.arange(top)[None, :] + offset_by) % top, axis=1)


def load_shares(number_of, total, reach, slope, full):
    weights = [(1 << 20) // math.isqrt(standing ** slope) + 1 for standing in range(1, number_of + 1)]
    largest = reach if full else min(reach, max(-(-total // number_of), total * weights[0] // sum(weights)))
    least = 1 if total - largest >= number_of - 1 else 0
    counts, rest = [largest] + [least] * (number_of - 1), total - largest - least * (number_of - 1)
    while rest > 0:
        movable = [i for i in range(1, number_of) if counts[i] < largest] or [i for i in range(1, number_of) if counts[i] < reach]
        mass, budget = sum([weights[i] for i in movable]), rest
        for i in movable:
            addition = min(reach - counts[i], max(1, budget * weights[i] // mass), rest)
            counts[i] = counts[i] + addition
            rest = rest - addition
    return np.array(counts)


def centred(rng, shape, scale, limit, cuts=(), kind=jnp.bfloat16):
    values = scale * jax.random.normal(rng, shape, jnp.float32)
    if cuts:
        values = values * level_of(rng, shape, cuts, -0.22, 0.18)
    return jnp.clip(values, -limit, limit).astype(kind)


def setup_inputs(seed: int = 0) -> dict:
    key_list = jax.random.split(jax.random.key(seed), 7)
    records = centred(key_list[0], (STATIONS, 3, DLEN), 1.0, 6.0, ((0, 128),))
    templates = centred(key_list[1], (TEMPLATES, PICKS, 3, TLEN), 1.0, 6.0, ((0, 128),))
    pick_owner_keys = jax.random.split(jax.random.fold_in(key_list[2], 1), TEMPLATES // TPL_LOC)
    pick_owner_turns = jax.random.permutation(jax.random.fold_in(key_list[2], 3), TEMPLATES // TPL_LOC)
    pick_owner = jax.vmap(lambda own, number: routed_block(jax.random.fold_in(key_list[2], 2), own, number, TPL_LOC, DEVICES, PICKS, CAP, 2))(pick_owner_keys, pick_owner_turns).reshape((TEMPLATES, PICKS))
    pick_local = set_ends(jax.random.randint(key_list[3], (TEMPLATES, PICKS), 0, STA_LOC), jax.random.fold_in(key_list[3], 1), 0, STA_LOC - 1).astype(jnp.int32)
    moveout = set_ends(jax.random.randint(key_list[4], (TEMPLATES, PICKS), 0, 128), jax.random.fold_in(key_list[4], 1), 0, 127).astype(jnp.int32)
    channel_mask = set_ends((jax.random.randint(key_list[5], (TEMPLATES, PICKS, 3), 0, 5) < 4).astype(jnp.int32), jax.random.fold_in(key_list[5], 1), 0, 1)
    return dict(records=records, templates=templates, pick_owner=pick_owner, pick_local=pick_local, moveout=moveout, channel_mask=channel_mask)


EPS = 1e-06

def reference(records, templates, pick_owner, pick_local, moveout, channel_mask):
    lag_span = LAGS + 128
    length = 2 ** int(math.ceil(math.log2(DLEN)))
    signal = records.astype(jnp.float32)
    spectra = jnp.fft.rfft(signal, n=length, axis=-1)
    energy = lax.reduce_window(signal * signal, jnp.zeros((), jnp.float32), lax.add, (1, 1, TLEN), (1, 1, 1), 'VALID')[:, :, :lag_span]
    station = pick_owner * STA_LOC + pick_local
    block_size = math.gcd(TEMPLATES, 64)
    block_total = TEMPLATES // block_size

    def per_block(pieces):
        shapes, stations, mask_rows, shifts = pieces
        shapes = shapes.astype(jnp.float32)
        template_spec = jnp.fft.rfft(shapes, n=length, axis=-1)
        correlated = jnp.fft.irfft(jnp.conj(template_spec) * spectra[stations], n=length, axis=-1)[..., :lag_span]
        template_power = lax.optimization_barrier(jnp.sum(shapes * shapes, axis=-1))[..., None]
        scaled = correlated * lax.rsqrt(template_power * energy[stations] + EPS)
        traces = lax.optimization_barrier(jnp.sum(mask_rows.astype(jnp.float32)[..., None] * scaled, axis=2)).astype(jnp.bfloat16)
        indices = shifts[..., None] + jnp.arange(LAGS, dtype=jnp.int32)[None, None, :]
        aligned = jnp.take_along_axis(traces, indices, axis=-1).astype(jnp.float32)
        stacked = lax.optimization_barrier(jnp.sum(aligned, axis=1))
        levels = jnp.sqrt(lax.optimization_barrier(jnp.mean(stacked * stacked, axis=-1, keepdims=True)) + EPS)
        return stacked / levels
    result = lax.map(per_block, (templates.reshape(block_total, block_size, PICKS, 3, TLEN), station.reshape(block_total, block_size, PICKS), channel_mask.reshape(block_total, block_size, PICKS, 3), moveout.reshape(block_total, block_size, PICKS)))
    return result.reshape(TEMPLATES, LAGS)
```

```python
import functools

import jax
import jax.numpy as jnp
from jax import lax
from jax.experimental import pallas as pl
from jax.experimental.pallas import tpu as pltpu
from jax.sharding import PartitionSpec as P

EPS = 1e-06
CAP = 3
SIDE = 4
UNROLL = 8
INFO = 8


def shifted(axis, step):
    if axis == "x":
        return [(x * SIDE + z, ((x + step) % SIDE) * SIDE + z) for x in range(SIDE) for z in range(SIDE)]
    return [(x * SIDE + z, x * SIDE + (z + step) % SIDE) for x in range(SIDE) for z in range(SIDE)]


def ring(block, axis):
    behind = lax.ppermute(block, "sta", shifted(axis, 1))
    ahead = lax.ppermute(block, "sta", shifted(axis, -1))
    half = block.shape[0] // 2
    far_a = lax.ppermute(behind[:half], "sta", shifted(axis, 1))
    far_b = lax.ppermute(ahead[half:], "sta", shifted(axis, -1))
    return behind, ahead, far_a, far_b


def pick_kernel(picks_per_source, taps, counts, info, power, inbox, *refs):
    piece_count = 10
    pieces = refs[:piece_count]
    out, records, frames, energy, total, shapes, wide, sums, sem = refs[piece_count:]
    copies = []
    base = 0
    for number, piece in enumerate(pieces):
        size = piece.shape[0]
        copies.append((base, size, pltpu.make_async_copy(piece, records.at[pl.ds(base, size)], sem.at[number])))
        base += size
    for _, _, copy in copies:
        copy.start()

    lanes = lax.broadcasted_iota(jnp.int32, (inbox.shape[0], 128), 1)
    for k in range(inbox.shape[1] // 128):
        block = inbox[:, k * 128 : k * 128 + 128].astype(jnp.float32)
        if k == 0:
            block = jnp.where(lanes < INFO, 0.0, block)
        shapes[pl.ds(k, inbox.shape[0], stride=8), :] = block
    total[...] = jnp.zeros_like(total)

    row = lax.broadcasted_iota(jnp.int32, (256, 384), 0)
    column = lax.broadcasted_iota(jnp.int32, (256, 384), 1)
    reach = (column // 128) * 128 + row % 128 - column % 128
    band = jnp.where((reach >= 0) & (reach < taps), 1.0, 0.0).astype(jnp.bfloat16)
    group = sums.shape[0] // 112

    def prepare(step, carry):
        x = records[pl.ds(step * group, group)].reshape(group * 112, 128).astype(jnp.float32)
        wide[...] = x
        square = x * x
        high = square.astype(jnp.bfloat16)
        low = (square - high.astype(jnp.float32)).astype(jnp.bfloat16)
        sums[...] = jnp.dot(jnp.concatenate([high, low], axis=1), band, preferred_element_type=jnp.float32)
        for s in range(group):
            for c in range(3):
                at = s * 112 + c * 35
                slot = (step * group + s) * 3 + c
                energy[slot] = (
                    sums[at : at + 40, 0:128] + sums[at + 1 : at + 41, 128:256] + sums[at + 2 : at + 42, 256:384]
                )
                for q in range(3):
                    frames[slot, 0:40, q * 128 : q * 128 + 128] = wide[at + q : at + q + 40, :].astype(jnp.bfloat16)
        return carry

    for first, size, copy in copies:
        copy.wait()
        lax.fori_loop(first // group, (first + size) // group, prepare, 0)

    across = lax.broadcasted_iota(jnp.int32, (128, 128), 1)
    below = across <= lax.broadcasted_iota(jnp.int32, (128, 128), 0)
    nothing = jnp.zeros((128, 128), jnp.bfloat16)
    lag = lax.broadcasted_iota(jnp.int32, (32, 128), 1)

    def spread(line):
        block = jnp.broadcast_to(line, (128, 128))
        return pltpu.roll(block, 1, 1, stride=1, stride_axis=0).astype(jnp.bfloat16)

    def one_pick(i):
        station, shift, target = info[INFO * i], info[INFO * i + 1], info[INFO * i + 2]
        trace = None
        lines = shapes[pl.ds(pl.multiple_of(8 * i, 8), 8), :]
        for c in range(3):
            late = spread(lines[2 * c : 2 * c + 1])
            early = spread(lines[2 * c + 1 : 2 * c + 2])
            toeplitz = jnp.concatenate(
                [jnp.where(below, early, nothing), jnp.where(below, late, early), jnp.where(below, nothing, late)],
                axis=0,
            )
            number = jnp.dot(frames[3 * station + c], toeplitz, preferred_element_type=jnp.float32)[:40]
            level = lax.rsqrt(power[4 * i + c] * energy[3 * station + c] + EPS)
            scaled = number * level * info[INFO * i + 3 + c].astype(jnp.float32)
            trace = scaled if trace is None else trace + scaled
        trace = trace.astype(jnp.bfloat16).astype(jnp.float32)
        turned = pltpu.roll(trace, 128 - shift, 1)
        following = pltpu.roll(turned, 39, 0)
        total[target] += jnp.where(lag < 128 - shift, turned[:32], following[:32])

    for source in range(out.shape[0] // 24):
        def several(step, carry):
            for u in range(UNROLL):
                one_pick(source * picks_per_source + step * UNROLL + u)
            return carry

        lax.fori_loop(0, (counts[source] + UNROLL - 1) // UNROLL, several, 0)
    out[...] = total[...].astype(out.dtype)


def stack_kernel(parts, out, total):
    rows = out.shape[0]
    summed = parts[0].astype(jnp.float32)
    for p in range(1, parts.shape[0]):
        summed = summed + parts[p].astype(jnp.float32)
    cube = summed.reshape(rows, 32, 128)
    square = jnp.sum(jnp.sum(cube * cube, axis=2, keepdims=True), axis=1, keepdims=True)
    level = jnp.sqrt(square / (32 * 128) + EPS)
    total[...] = (cube / level).reshape(rows * 32, 128)
    for b in range(32):
        out[:, b * 128 : b * 128 + 128] = total[pl.ds(b, rows, stride=32), :]


def on_device(records, templates, pick_owner, pick_local, moveout, channel_mask):
    own_templates, pick_count, channels, taps = templates.shape
    columns = lax.axis_size("tpl")
    lines = lax.axis_size("sta")
    rows = own_templates * pick_count
    per_source = CAP * lines
    slots = columns * per_source
    stations = lines * records.shape[0]
    vmem, smem = pl.BlockSpec(memory_space=pltpu.VMEM), pl.BlockSpec(memory_space=pltpu.SMEM)

    pieces = records.reshape(records.shape[0], 105, 128)
    pieces = jnp.pad(pieces, ((0, 0), (0, 7), (0, 0)))
    half = records.shape[0] // 2
    by_x = jnp.concatenate((pieces[:half],) + ring(pieces[:half], "x"))
    by_z = jnp.concatenate((pieces[half:],) + ring(pieces[half:], "z"))
    gathered = (by_x,) + ring(by_x, "z") + (by_z,) + ring(by_z, "x")

    here = lax.axis_index("sta")
    owner = pick_owner.reshape(rows)
    line, column = owner // columns, owner % columns
    ahead_x = (line // SIDE - here // SIDE) % SIDE
    ahead_z = (line % SIDE - here % SIDE) % SIDE
    order_x = jnp.where(ahead_x == 3, 1, jnp.where(ahead_x == 0, 0, ahead_x + 1))
    order_z = jnp.where(ahead_z == 3, 1, jnp.where(ahead_z == 0, 0, ahead_z + 1))
    local = pick_local.reshape(rows)
    station = jnp.where(
        local < half,
        16 * order_z + 4 * order_x + local,
        64 + 16 * order_x + 4 * order_z + local - half,
    )
    onehot = (column[:, None] == jnp.arange(columns, dtype=jnp.int32)[None, :]).astype(jnp.int32)
    before = jnp.cumsum(onehot, axis=0) - onehot
    position = column * per_source + jnp.sum(before * onehot, axis=1)
    target = jnp.arange(rows, dtype=jnp.int32) // pick_count
    details = jnp.concatenate(
        [
            station[:, None],
            moveout.reshape(rows, 1),
            target[:, None],
            channel_mask.reshape(rows, channels),
            jnp.ones((rows, 1), jnp.int32),
        ],
        axis=1,
    ).astype(jnp.bfloat16)
    front = jnp.pad(details, ((0, 0), (0, 56 - details.shape[1])))[:, None, :]
    front = jnp.pad(front, ((0, 0), (0, channels - 1), (0, 0)))
    sent = jnp.concatenate([front, templates.reshape(rows, channels, taps)[:, :, ::-1]], axis=2)
    place = (position[None, :] == jnp.arange(slots, dtype=jnp.int32)[:, None]).astype(jnp.bfloat16)
    outbox = jnp.dot(place, sent.reshape(rows, channels * 256), preferred_element_type=jnp.float32)
    inbox = lax.all_to_all(
        outbox.astype(jnp.bfloat16).reshape(columns, per_source, channels * 256),
        "tpl",
        split_axis=0,
        concat_axis=0,
        tiled=True,
    )
    marks = inbox[:, :, :INFO].astype(jnp.int32)
    counts = jnp.sum(marks[:, :, 6], axis=1)
    offset = own_templates * jnp.arange(columns, dtype=jnp.int32)[:, None]
    marks = marks.at[:, :, 2].add(offset).reshape(slots * INFO)
    inbox = inbox.reshape(slots, channels * 256)
    wide = inbox.reshape(slots, channels, 256)[:, :, 56:].astype(jnp.float32)
    power = jnp.pad(jnp.sum(wide * wide, axis=2), ((0, 0), (0, 1))).reshape(slots * 4)

    total_rows = columns * own_templates
    partial = pl.pallas_call(
        functools.partial(pick_kernel, per_source, taps),
        out_shape=jax.ShapeDtypeStruct((total_rows, 32, 128), jnp.bfloat16),
        in_specs=[smem, smem, smem, vmem] + [pl.BlockSpec(memory_space=pl.ANY)] * len(gathered),
        out_specs=vmem,
        scratch_shapes=[
            pltpu.VMEM((stations, 112, 128), jnp.bfloat16),
            pltpu.VMEM((stations * 3, 48, 384), jnp.bfloat16),
            pltpu.VMEM((stations * 3, 40, 128), jnp.float32),
            pltpu.VMEM((total_rows, 32, 128), jnp.float32),
            pltpu.VMEM((slots * 8, 128), jnp.float32),
            pltpu.VMEM((8 * 112, 128), jnp.float32),
            pltpu.VMEM((8 * 112, 384), jnp.float32),
            pltpu.SemaphoreType.DMA((len(gathered),)),
        ],
        compiler_params=pltpu.CompilerParams(vmem_limit_bytes=56 * 2**20),
    )(counts, marks, power, inbox, *gathered)

    returned = lax.all_to_all(
        partial.reshape(columns, own_templates * 32, 128), "tpl", split_axis=0, concat_axis=0, tiled=True
    )
    return pl.pallas_call(
        stack_kernel,
        out_shape=jax.ShapeDtypeStruct((own_templates, 4096), jnp.float32),
        in_specs=[vmem],
        out_specs=vmem,
        scratch_shapes=[pltpu.VMEM((own_templates * 32, 128), jnp.float32)],
        compiler_params=pltpu.CompilerParams(vmem_limit_bytes=32 * 2**20),
    )(returned)


def solution(mesh):
    return jax.shard_map(
        on_device,
        mesh=mesh,
        in_specs=(
            P(("sta", "tpl"), None, None),
            P(("sta", "tpl"), None, None, None),
            P(("sta", "tpl"), None),
            P(("sta", "tpl"), None),
            P(("sta", "tpl"), None),
            P(("sta", "tpl"), None, None),
        ),
        out_specs=P(("sta", "tpl"), None),
        check_vma=False,
    )
```

```python
import functools

import jax
import jax.numpy as jnp
from jax import lax
from jax.experimental import pallas as pl
from jax.experimental.pallas import tpu as pltpu
from jax.sharding import PartitionSpec as P

EPS = 1e-06
CAP = 3
SIDE = 4
UNROLL = 16
INFO = 16
PIECES = (2, 2, 4)
FIRST = (0, 32, 64)
STATIONS = (32, 32, 64)


def shifted(axis, step):
    if axis == "x":
        return [(x * SIDE + z, ((x + step) % SIDE) * SIDE + z) for x in range(SIDE) for z in range(SIDE)]
    return [(x * SIDE + z, x * SIDE + (z + step) % SIDE) for x in range(SIDE) for z in range(SIDE)]


def after_kernel(first, second, token, same_first, same_second):
    pass


def ring(first, second, axis, between=None):
    behind_first = lax.ppermute(first, "sta", shifted(axis, 1))
    ahead_second = lax.ppermute(second, "sta", shifted(axis, -1))
    behind_second = lax.ppermute(second, "sta", shifted(axis, 1))
    ahead_first = lax.ppermute(first, "sta", shifted(axis, -1))
    if between is not None:
        behind_first, ahead_second = between(behind_first, ahead_second)
    far_first = lax.ppermute(behind_first, "sta", shifted(axis, 1))
    far_second = lax.ppermute(ahead_second, "sta", shifted(axis, -1))
    return behind_first, behind_second, ahead_first, ahead_second, far_first, far_second


def front_kernel(per_source, here, owner, local, shift, mask, templates, records, outbox, pieces, spread):
    pick_count, channels, own_templates, taps = templates.shape
    rows = pick_count * own_templates
    for c in range(channels):
        for b in range(35):
            block = records[c, :, b * 128 : b * 128 + 128].astype(jnp.float32)
            spread[pl.ds(c * 35 + b, 8, stride=112), :] = block
    for b in range(105, 112):
        spread[pl.ds(b, 8, stride=112), :] = jnp.zeros((8, 128), jnp.float32)
    pieces[...] = spread[...].reshape(pieces.shape).astype(pieces.dtype)

    def flat(table):
        return jnp.concatenate([table[p : p + 1] for p in range(pick_count)], axis=1)

    owner, local, shift = flat(owner[...]), flat(local[...]), flat(shift[...])
    line, column = owner >> 3, owner & 7
    ahead_x = ((line >> 2) - (here[0] >> 2)) & 3
    ahead_z = ((line & 3) - (here[0] & 3)) & 3
    order_x = jnp.where(ahead_x == 3, 1, jnp.where(ahead_x == 0, 0, ahead_x + 1))
    order_z = jnp.where(ahead_z == 3, 1, jnp.where(ahead_z == 0, 0, ahead_z + 1))
    near = 8 * order_x + local
    early = jnp.where(near < 16, 1, 2) == order_z
    stage = jnp.where(order_z == 0, 0, jnp.where(early, 1, 2))
    late = near + jnp.where(order_z == 1, 48, jnp.where(order_z == 2, 80, 96))
    station = jnp.where(stage == 0, near, jnp.where(early, 32 + near, late))
    bins = lax.broadcasted_iota(jnp.int32, (128, rows), 0)
    own = 3 * column + stage == bins
    hot = jnp.where(own, 1.0, 0.0)
    upper = lax.broadcasted_iota(jnp.int32, (rows, rows), 0) < lax.broadcasted_iota(jnp.int32, (rows, rows), 1)
    upper = jnp.where(upper, 1.0, 0.0).astype(jnp.bfloat16)
    before = jnp.dot(hot.astype(jnp.bfloat16), upper, preferred_element_type=jnp.float32)
    held = jnp.broadcast_to(jnp.sum(hot, axis=1, keepdims=True), (128, 128))
    i = lax.broadcasted_iota(jnp.int32, (128, 128), 0)
    j = lax.broadcasted_iota(jnp.int32, (128, 128), 1)
    earlier = jnp.where((((i * 43) >> 7) == ((j * 43) >> 7)) & (j < i), 1.0, 0.0).astype(jnp.bfloat16)
    starts = jnp.dot(earlier, held.astype(jnp.bfloat16), preferred_element_type=jnp.float32)[:, 0:1]
    rank = jnp.sum(jnp.where(own, before + starts, 0.0), axis=0, keepdims=True).astype(jnp.int32)
    position = column * per_source + rank
    template = lax.broadcasted_iota(jnp.int32, (1, rows), 1)
    template = template - own_templates * ((template * 683) >> 14)
    facts = [station, shift, template] + [flat(mask[:, c, :]) for c in range(channels)]
    facts = [fact.astype(jnp.float32) for fact in facts] + [jnp.ones((1, rows), jnp.float32)]
    for k in range(3):
        facts.append(jnp.sum(jnp.where(bins == 3 * column + k, held[:, 0:1], 0.0), axis=0, keepdims=True))
    facts.append(jnp.zeros((16 - len(facts), rows), jnp.float32))
    facts = jnp.concatenate(facts, axis=0).astype(jnp.bfloat16)
    slot = lax.broadcasted_iota(jnp.int32, (outbox.shape[0], rows), 0)
    place = jnp.where(position == slot, 1.0, 0.0).astype(jnp.bfloat16)
    i = lax.broadcasted_iota(jnp.int32, (taps, 256), 0)
    j = lax.broadcasted_iota(jnp.int32, (taps, 256), 1)
    turn = jnp.where(i == 255 - j, 1.0, 0.0).astype(jnp.bfloat16)
    for c in range(channels):
        block = templates[:, c].reshape(rows, taps)
        sent = jnp.dot(block, turn, preferred_element_type=jnp.float32).astype(jnp.bfloat16)
        placed = jnp.dot(place, sent, preferred_element_type=jnp.float32)
        if c == 0:
            i = lax.broadcasted_iota(jnp.int32, (16, 256), 0)
            j = lax.broadcasted_iota(jnp.int32, (16, 256), 1)
            lead = jnp.where(i == j, 1.0, 0.0).astype(jnp.bfloat16)
            known = lax.dot_general(place, facts, (((1,), (1,)), ((), ())), preferred_element_type=jnp.float32)
            placed = placed + jnp.dot(known.astype(jnp.bfloat16), lead, preferred_element_type=jnp.float32)
        outbox[:, 256 * c : 256 * c + 256] = placed.astype(jnp.bfloat16)


def unpack_kernel(inbox, first, second, shapes, marks, power, same_first, same_second):
    slots = inbox.shape[0]
    lanes = lax.broadcasted_iota(jnp.int32, (slots, 128), 1)
    info = inbox[:, 0:128].astype(jnp.float32)
    zero = jnp.zeros((16, 128), jnp.int32)
    for k in range(slots // 128):
        turned = jnp.transpose(info[k * 128 : k * 128 + 128])[:16].astype(jnp.int32)
        marks[:, k * 128 : k * 128 + 128] = turned
    marks[:, slots : slots + 128] = zero
    shapes[pl.ds(8 * slots, 8), :] = jnp.zeros((8, 128), jnp.float32)
    square = jnp.zeros((slots, 128), jnp.float32)
    for k in range(inbox.shape[1] // 128):
        block = inbox[:, k * 128 : k * 128 + 128].astype(jnp.float32)
        if k == 0:
            block = jnp.where(lanes < INFO, 0.0, block)
        shapes[pl.ds(k, slots, stride=8), :] = block
        square = jnp.where(lanes == k // 2, square + jnp.sum(block * block, axis=1, keepdims=True), square)
    for k in range(slots // 128):
        power[:, k * 128 : k * 128 + 128] = jnp.transpose(square[k * 128 : k * 128 + 128])[:8]
    power[:, slots : slots + 128] = jnp.zeros((8, 128), jnp.float32)


def pick_kernel(stage, per_source, taps, marks, power, shapes, *refs):
    pieces = refs[: PIECES[stage]]
    refs = refs[PIECES[stage] :]
    if stage > 0:
        refs = refs[1:]
    total, extra, records, frames, energy, wide, sums, order, sem = refs
    copies = []
    base = 0
    for number, piece in enumerate(pieces):
        size = piece.shape[0]
        copies.append((base, size, pltpu.make_async_copy(piece, records.at[pl.ds(base, size)], sem.at[number])))
        base += size
    for _, _, copy in copies:
        copy.start()
    if stage == 0:
        total[...] = jnp.zeros_like(total)

    taken = jnp.int32(0)
    for source in range(total.shape[0] // 24):
        first = jnp.int32(source * per_source)
        for earlier in range(stage):
            first = first + marks[7 + earlier, source * per_source]
        count = marks[7 + stage, source * per_source]

        def note(k, carry, first=first, taken=taken):
            order[taken + k] = first + k
            return carry

        lax.fori_loop(0, count, note, 0)
        taken = taken + count
    for u in range(UNROLL):
        order[taken + u] = jnp.int32(marks.shape[1] - 128)

    row = lax.broadcasted_iota(jnp.int32, (256, 384), 0)
    column = lax.broadcasted_iota(jnp.int32, (256, 384), 1)
    reach = (column // 128) * 128 + row % 128 - column % 128
    band = jnp.where((reach >= 0) & (reach < taps), 1.0, 0.0).astype(jnp.bfloat16)
    group = sums.shape[0] // 112

    def prepare(step, carry):
        x = records[pl.ds(step * group, group)].reshape(group * 112, 128).astype(jnp.float32)
        wide[...] = x
        square = x * x
        high = square.astype(jnp.bfloat16)
        low = (square - high.astype(jnp.float32)).astype(jnp.bfloat16)
        sums[...] = jnp.dot(jnp.concatenate([high, low], axis=1), band, preferred_element_type=jnp.float32)
        for s in range(group):
            for c in range(3):
                at = s * 112 + c * 35
                slot = (step * group + s) * 3 + c
                energy[slot] = (
                    sums[at : at + 40, 0:128] + sums[at + 1 : at + 41, 128:256] + sums[at + 2 : at + 42, 256:384]
                )
                for q in range(3):
                    frames[slot, 0:40, q * 128 : q * 128 + 128] = wide[at + q : at + q + 40, :].astype(jnp.bfloat16)
        return carry

    for first, size, copy in copies:
        copy.wait()
        lax.fori_loop(first // group, (first + size) // group, prepare, 0)

    across = lax.broadcasted_iota(jnp.int32, (128, 128), 1)
    below = across <= lax.broadcasted_iota(jnp.int32, (128, 128), 0)
    nothing = jnp.zeros((128, 128), jnp.bfloat16)
    lag = lax.broadcasted_iota(jnp.int32, (32, 128), 1)

    def spread(line):
        block = jnp.broadcast_to(line, (128, 128))
        return pltpu.roll(block, 1, 1, stride=1, stride_axis=0).astype(jnp.bfloat16)

    def one_pick(i):
        station = 3 * jnp.maximum(marks[0, i] - FIRST[stage], 0)
        shift = marks[1, i]
        target = marks[2, i] + 24 * jnp.minimum(i // per_source, 7)
        trace = None
        lines = shapes[pl.ds(pl.multiple_of(8 * i, 8), 8), :]
        for c in range(3):
            late = spread(lines[2 * c : 2 * c + 1])
            early = spread(lines[2 * c + 1 : 2 * c + 2])
            toeplitz = jnp.concatenate(
                [jnp.where(below, early, nothing), jnp.where(below, late, early), jnp.where(below, nothing, late)],
                axis=0,
            )
            number = jnp.dot(frames[station + c], toeplitz, preferred_element_type=jnp.float32)[:40]
            level = lax.rsqrt(power[c, i] * energy[station + c] + EPS)
            scaled = number * level * marks[3 + c, i].astype(jnp.float32)
            trace = scaled if trace is None else trace + scaled
        trace = trace.astype(jnp.bfloat16).astype(jnp.float32)
        turned = pltpu.roll(trace, 128 - shift, 1)
        following = pltpu.roll(turned, 39, 0)
        total[target] += jnp.where(lag < 128 - shift, turned[:32], following[:32])

    def several(step, carry):
        for u in range(UNROLL):
            one_pick(order[step * UNROLL + u])
        return carry

    whole = taken // UNROLL
    lax.fori_loop(0, whole, several, 0)

    def rest(step, carry):
        for u in range(4):
            one_pick(order[step * 4 + u])
        return carry

    lax.fori_loop(whole * (UNROLL // 4), (taken + 3) // 4, rest, 0)
    extra[...] = total[: extra.shape[0]].astype(extra.dtype)


def stack_kernel(parts, out, total):
    rows = out.shape[0]
    summed = parts[0].astype(jnp.float32)
    for p in range(1, parts.shape[0]):
        summed = summed + parts[p].astype(jnp.float32)
    cube = summed.reshape(rows, 32, 128)
    square = jnp.sum(jnp.sum(cube * cube, axis=2, keepdims=True), axis=1, keepdims=True)
    level = jnp.sqrt(square / (32 * 128) + EPS)
    total[...] = (cube / level).reshape(rows * 32, 128)
    for b in range(32):
        out[:, b * 128 : b * 128 + 128] = total[pl.ds(b, rows, stride=32), :]


def on_device(records, templates, pick_owner, pick_local, moveout, channel_mask):
    own_templates, pick_count, channels, taps = templates.shape
    columns = lax.axis_size("tpl")
    lines = lax.axis_size("sta")
    rows = own_templates * pick_count
    per_source = CAP * lines
    slots = columns * per_source
    anywhere = pl.BlockSpec(memory_space=pl.ANY)
    vmem, smem = pl.BlockSpec(memory_space=pltpu.VMEM), pl.BlockSpec(memory_space=pltpu.SMEM)

    here = lax.axis_index("sta").astype(jnp.int32).reshape(1)
    outbox, pieces = pl.pallas_call(
        functools.partial(front_kernel, per_source),
        out_shape=(
            jax.ShapeDtypeStruct((slots, channels * 256), jnp.bfloat16),
            jax.ShapeDtypeStruct((records.shape[0], 112, 128), jnp.bfloat16),
        ),
        in_specs=[smem] + [vmem] * 6,
        out_specs=(vmem, vmem),
        scratch_shapes=[pltpu.VMEM((records.shape[0] * 112, 128), jnp.float32)],
        compiler_params=pltpu.CompilerParams(vmem_limit_bytes=60 * 2**20),
    )(
        here,
        pick_owner.T,
        pick_local.T,
        moveout.T,
        channel_mask.transpose(1, 2, 0),
        templates.transpose(1, 2, 0, 3),
        records.transpose(1, 0, 2),
    )
    half = records.shape[0] // 2
    around = ring(pieces[:half], pieces[half:], "x")
    near_first = jnp.concatenate((pieces,) + around[:2])
    near_second = jnp.concatenate(around[2:])
    inbox = lax.all_to_all(
        outbox.reshape(columns, per_source, channels * 256),
        "tpl",
        split_axis=0,
        concat_axis=0,
        tiled=True,
    )
    total_rows = columns * own_templates
    shapes, marks, power, near_first, near_second = pl.pallas_call(
        unpack_kernel,
        out_shape=(
            pltpu.VMEM((slots * 8 + 8, 128), jnp.float32),
            jax.ShapeDtypeStruct((16, slots + 128), jnp.int32),
            jax.ShapeDtypeStruct((8, slots + 128), jnp.float32),
            jax.ShapeDtypeStruct(near_first.shape, near_first.dtype),
            jax.ShapeDtypeStruct(near_second.shape, near_second.dtype),
        ),
        in_specs=[vmem, anywhere, anywhere],
        out_specs=(vmem, vmem, vmem, anywhere, anywhere),
        input_output_aliases={1: 3, 2: 4},
        compiler_params=pltpu.CompilerParams(vmem_limit_bytes=20 * 2**20),
    )(inbox.reshape(slots, channels * 256), near_first, near_second)
    shapes = pltpu.with_memory_space_constraint(shapes, pltpu.VMEM)

    def run_stage(stage, gathered, carried):
        scratch = [
            pltpu.VMEM((STATIONS[stage], 112, 128), jnp.bfloat16),
            pltpu.VMEM((STATIONS[stage] * 3, 48, 384), jnp.bfloat16),
            pltpu.VMEM((STATIONS[stage] * 3, 40, 128), jnp.float32),
            pltpu.VMEM((16 * 112, 128), jnp.float32),
            pltpu.VMEM((16 * 112, 384), jnp.float32),
            pltpu.SMEM((slots + 128,), jnp.int32),
            pltpu.SemaphoreType.DMA((PIECES[stage],)),
        ]
        result = pltpu.VMEM((total_rows, 32, 128), jnp.float32)
        extra = jax.ShapeDtypeStruct((total_rows if stage == 2 else 1, 32, 128), jnp.bfloat16)
        carried = [pltpu.with_memory_space_constraint(p, pltpu.VMEM) for p in carried]
        return pl.pallas_call(
            functools.partial(pick_kernel, stage, per_source, taps),
            out_shape=(result, extra),
            in_specs=[smem, smem, vmem] + [anywhere] * PIECES[stage] + [vmem] * len(carried),
            out_specs=(vmem, vmem),
            scratch_shapes=scratch,
            input_output_aliases={3 + PIECES[stage]: 0} if carried else {},
            cost_estimate=pl.CostEstimate(flops=0, bytes_accessed=(30, 50, 30)[stage] * 10**6, transcendentals=0),
            compiler_params=pltpu.CompilerParams(vmem_limit_bytes=48 * 2**20),
        )(marks, power, shapes, *gathered, *carried)

    partial, token = run_stage(0, (near_first, near_second), ())

    def after(first, second):
        return pl.pallas_call(
            after_kernel,
            out_shape=tuple(jax.ShapeDtypeStruct(x.shape, x.dtype) for x in (first, second)),
            in_specs=[anywhere] * 3,
            out_specs=(anywhere, anywhere),
            input_output_aliases={0: 0, 1: 1},
            compiler_params=pltpu.CompilerParams(vmem_limit_bytes=2**20),
        )(first, second, token)

    far = ring(near_first, near_second, "z", after)
    partial, _ = run_stage(1, (far[0], far[3]), (partial,))
    _, partial = run_stage(2, (far[1], far[2], far[4], far[5]), (partial,))

    returned = lax.all_to_all(
        partial.reshape(columns, own_templates * 32, 128), "tpl", split_axis=0, concat_axis=0, tiled=True
    )
    return pl.pallas_call(
        stack_kernel,
        out_shape=jax.ShapeDtypeStruct((own_templates, 4096), jnp.float32),
        in_specs=[vmem],
        out_specs=vmem,
        scratch_shapes=[pltpu.VMEM((own_templates * 32, 128), jnp.float32)],
        compiler_params=pltpu.CompilerParams(vmem_limit_bytes=20 * 2**20),
    )(returned)


def solution(mesh):
    return jax.shard_map(
        on_device,
        mesh=mesh,
        in_specs=(
            P(("sta", "tpl"), None, None),
            P(("sta", "tpl"), None, None, None),
            P(("sta", "tpl"), None),
            P(("sta", "tpl"), None),
            P(("sta", "tpl"), None),
            P(("sta", "tpl"), None, None),
        ),
        out_specs=P(("sta", "tpl"), None),
        check_vma=False,
    )
```

```python
import functools

import jax
import jax.numpy as jnp
from jax import lax
from jax.experimental import pallas as pl
from jax.experimental.pallas import tpu as pltpu
from jax.sharding import PartitionSpec as P

EPS = 1e-06
CAP = 3
SIDE = 4
UNROLL = 16
INFO = 16
PIECES = (2, 2, 2, 2)
FIRST = (0, 32, 64, 96)
STATIONS = (32, 32, 32, 32)


def shifted(axis, step):
    if axis == "x":
        return [(x * SIDE + z, ((x + step) % SIDE) * SIDE + z) for x in range(SIDE) for z in range(SIDE)]
    return [(x * SIDE + z, x * SIDE + (z + step) % SIDE) for x in range(SIDE) for z in range(SIDE)]


def after_kernel(first, second, token, same_first, same_second):
    pass


def ring(first, second, axis, between=None):
    behind_first = lax.ppermute(first, "sta", shifted(axis, 1))
    ahead_second = lax.ppermute(second, "sta", shifted(axis, -1))
    behind_second = lax.ppermute(second, "sta", shifted(axis, 1))
    ahead_first = lax.ppermute(first, "sta", shifted(axis, -1))
    if between is not None:
        behind_first, ahead_second = between(behind_first, ahead_second)
    far_first = lax.ppermute(behind_first, "sta", shifted(axis, 1))
    far_second = lax.ppermute(ahead_second, "sta", shifted(axis, -1))
    return behind_first, behind_second, ahead_first, ahead_second, far_first, far_second


def front_kernel(per_source, here, owner, local, shift, mask, templates, records, outbox, first, second, spread):
    pick_count, channels, own_templates, taps = templates.shape
    rows = pick_count * own_templates
    for c in range(channels):
        for b in range(35):
            block = records[c, :, b * 128 : b * 128 + 128].astype(jnp.float32)
            spread[pl.ds(c * 35 + b, 8, stride=112), :] = block
    for b in range(105, 112):
        spread[pl.ds(b, 8, stride=112), :] = jnp.zeros((8, 128), jnp.float32)
    half = first.shape[0] * 112
    first[...] = spread[:half].reshape(first.shape).astype(first.dtype)
    second[...] = spread[half:].reshape(second.shape).astype(second.dtype)

    def flat(table):
        return jnp.concatenate([table[p : p + 1] for p in range(pick_count)], axis=1)

    owner, local, shift = flat(owner[...]), flat(local[...]), flat(shift[...])
    line, column = owner >> 3, owner & 7
    ahead_x = ((line >> 2) - (here[0] >> 2)) & 3
    ahead_z = ((line & 3) - (here[0] & 3)) & 3
    order_x = jnp.where(ahead_x == 3, 1, jnp.where(ahead_x == 0, 0, ahead_x + 1))
    order_z = jnp.where(ahead_z == 3, 1, jnp.where(ahead_z == 0, 0, ahead_z + 1))
    near = 8 * order_x + local
    early = jnp.where(near < 16, 1, 2) == order_z
    stage = jnp.where(order_z == 0, 0, jnp.where(early, 1, jnp.where(order_z == 3, 3, 2)))
    late = near + jnp.where(order_z == 1, 48, jnp.where(order_z == 2, 80, 96))
    station = jnp.where(stage == 0, near, jnp.where(early, 32 + near, late))
    bins = lax.broadcasted_iota(jnp.int32, (128, rows), 0)
    own = 4 * column + stage == bins
    hot = jnp.where(own, 1.0, 0.0)
    upper = lax.broadcasted_iota(jnp.int32, (rows, rows), 0) < lax.broadcasted_iota(jnp.int32, (rows, rows), 1)
    upper = jnp.where(upper, 1.0, 0.0).astype(jnp.bfloat16)
    before = jnp.dot(hot.astype(jnp.bfloat16), upper, preferred_element_type=jnp.float32)
    held = jnp.broadcast_to(jnp.sum(hot, axis=1, keepdims=True), (128, 128))
    i = lax.broadcasted_iota(jnp.int32, (128, 128), 0)
    j = lax.broadcasted_iota(jnp.int32, (128, 128), 1)
    earlier = jnp.where(((i >> 2) == (j >> 2)) & (j < i), 1.0, 0.0).astype(jnp.bfloat16)
    starts = jnp.dot(earlier, held.astype(jnp.bfloat16), preferred_element_type=jnp.float32)[:, 0:1]
    rank = jnp.sum(jnp.where(own, before + starts, 0.0), axis=0, keepdims=True).astype(jnp.int32)
    position = column * per_source + rank
    template = lax.broadcasted_iota(jnp.int32, (1, rows), 1)
    template = template - own_templates * ((template * 683) >> 14)
    facts = [station, shift, template] + [flat(mask[:, c, :]) for c in range(channels)]
    facts = [fact.astype(jnp.float32) for fact in facts] + [jnp.ones((1, rows), jnp.float32)]
    for k in range(4):
        facts.append(jnp.sum(jnp.where(bins == 4 * column + k, held[:, 0:1], 0.0), axis=0, keepdims=True))
    facts.append(jnp.zeros((16 - len(facts), rows), jnp.float32))
    facts = jnp.concatenate(facts, axis=0).astype(jnp.bfloat16)
    slot = lax.broadcasted_iota(jnp.int32, (outbox.shape[0], rows), 0)
    place = jnp.where(position == slot, 1.0, 0.0).astype(jnp.bfloat16)
    i = lax.broadcasted_iota(jnp.int32, (taps, 256), 0)
    j = lax.broadcasted_iota(jnp.int32, (taps, 256), 1)
    turn = jnp.where(i == 255 - j, 1.0, 0.0).astype(jnp.bfloat16)
    for c in range(channels):
        block = templates[:, c].reshape(rows, taps)
        sent = jnp.dot(block, turn, preferred_element_type=jnp.float32).astype(jnp.bfloat16)
        placed = jnp.dot(place, sent, preferred_element_type=jnp.float32)
        if c == 0:
            i = lax.broadcasted_iota(jnp.int32, (16, 256), 0)
            j = lax.broadcasted_iota(jnp.int32, (16, 256), 1)
            lead = jnp.where(i == j, 1.0, 0.0).astype(jnp.bfloat16)
            known = lax.dot_general(place, facts, (((1,), (1,)), ((), ())), preferred_element_type=jnp.float32)
            placed = placed + jnp.dot(known.astype(jnp.bfloat16), lead, preferred_element_type=jnp.float32)
        outbox[:, 256 * c : 256 * c + 256] = placed.astype(jnp.bfloat16)


def unpack_kernel(inbox, first, second, shapes, marks, power, same_first, same_second):
    slots = inbox.shape[0]
    lanes = lax.broadcasted_iota(jnp.int32, (slots, 128), 1)
    info = inbox[:, 0:128].astype(jnp.float32)
    zero = jnp.zeros((16, 128), jnp.int32)
    for k in range(slots // 128):
        turned = jnp.transpose(info[k * 128 : k * 128 + 128])[:16].astype(jnp.int32)
        marks[:, k * 128 : k * 128 + 128] = turned
    marks[:, slots : slots + 128] = zero
    shapes[pl.ds(8 * slots, 8), :] = jnp.zeros((8, 128), jnp.float32)
    square = jnp.zeros((slots, 128), jnp.float32)
    for k in range(inbox.shape[1] // 128):
        block = inbox[:, k * 128 : k * 128 + 128].astype(jnp.float32)
        if k == 0:
            block = jnp.where(lanes < INFO, 0.0, block)
        shapes[pl.ds(k, slots, stride=8), :] = block
        square = jnp.where(lanes == k // 2, square + jnp.sum(block * block, axis=1, keepdims=True), square)
    for k in range(slots // 128):
        power[:, k * 128 : k * 128 + 128] = jnp.transpose(square[k * 128 : k * 128 + 128])[:8]
    power[:, slots : slots + 128] = jnp.zeros((8, 128), jnp.float32)


def pick_kernel(stage, per_source, taps, marks, power, shapes, *refs):
    pieces = refs[: PIECES[stage]]
    refs = refs[PIECES[stage] :]
    if stage > 0:
        refs = refs[1:]
    total, extra, records, frames, energy, wide, sums, order, sem = refs
    copies = []
    base = 0
    for number, piece in enumerate(pieces):
        size = piece.shape[0]
        copies.append((base, size, pltpu.make_async_copy(piece, records.at[pl.ds(base, size)], sem.at[number])))
        base += size
    for _, _, copy in copies:
        copy.start()
    if stage == 0:
        total[...] = jnp.zeros_like(total)

    taken = jnp.int32(0)
    for source in range(total.shape[0] // 24):
        first = jnp.int32(source * per_source)
        for earlier in range(stage):
            first = first + marks[7 + earlier, source * per_source]
        count = marks[7 + stage, source * per_source]

        def note(k, carry, first=first, taken=taken):
            order[taken + k] = first + k
            return carry

        lax.fori_loop(0, count, note, 0)
        taken = taken + count
    for u in range(UNROLL):
        order[taken + u] = jnp.int32(marks.shape[1] - 128)

    row = lax.broadcasted_iota(jnp.int32, (256, 256), 0) % 128
    column = lax.broadcasted_iota(jnp.int32, (256, 256), 1) % 128
    tail = taps - 128
    suffix = row >= column
    prefix = ((column < 128 - tail) & (row - column < tail)) | (column - row > 128 - tail)
    left = lax.broadcasted_iota(jnp.int32, (256, 256), 1) < 128
    band = jnp.where((left & suffix) | (~left & prefix), 1.0, 0.0).astype(jnp.bfloat16)
    near_side = lax.broadcasted_iota(jnp.int32, (40, 128), 1) < 128 - tail
    group = sums.shape[0] // 112

    def prepare(step, carry):
        x = records[pl.ds(step * group, group)].reshape(group * 112, 128).astype(jnp.float32)
        wide[...] = x
        square = x * x
        high = square.astype(jnp.bfloat16)
        low = (square - high.astype(jnp.float32)).astype(jnp.bfloat16)
        sums[...] = jnp.dot(jnp.concatenate([high, low], axis=1), band, preferred_element_type=jnp.float32)
        for s in range(group):
            for c in range(3):
                at = s * 112 + c * 35
                slot = (step * group + s) * 3 + c
                whole = jnp.broadcast_to(sums[at + 1 : at + 41, 0:128][:, 0:1], (40, 128))
                ending = jnp.where(
                    near_side, sums[at + 1 : at + 41, 128:256], whole + sums[at + 2 : at + 42, 128:256]
                )
                energy[slot] = sums[at : at + 40, 0:128] + ending
                for q in range(3):
                    frames[slot, 0:40, q * 128 : q * 128 + 128] = wide[at + q : at + q + 40, :].astype(jnp.bfloat16)
        return carry

    for first, size, copy in copies:
        copy.wait()
        lax.fori_loop(first // group, (first + size) // group, prepare, 0)

    across = lax.broadcasted_iota(jnp.int32, (128, 128), 1)
    below = across <= lax.broadcasted_iota(jnp.int32, (128, 128), 0)
    nothing = jnp.zeros((128, 128), jnp.bfloat16)
    lag = lax.broadcasted_iota(jnp.int32, (32, 128), 1)

    def spread(line):
        block = jnp.broadcast_to(line, (128, 128))
        return pltpu.roll(block, 1, 1, stride=1, stride_axis=0).astype(jnp.bfloat16)

    def one_pick(i):
        station = 3 * jnp.maximum(marks[0, i] - FIRST[stage], 0)
        shift = marks[1, i]
        target = marks[2, i] + 24 * jnp.minimum(i // per_source, 7)
        trace = None
        lines = shapes[pl.ds(pl.multiple_of(8 * i, 8), 8), :]
        for c in range(3):
            late = spread(lines[2 * c : 2 * c + 1])
            early = spread(lines[2 * c + 1 : 2 * c + 2])
            toeplitz = jnp.concatenate(
                [jnp.where(below, early, nothing), jnp.where(below, late, early), jnp.where(below, nothing, late)],
                axis=0,
            )
            number = jnp.dot(frames[station + c], toeplitz, preferred_element_type=jnp.float32)[:40]
            level = lax.rsqrt(power[c, i] * energy[station + c] + EPS)
            scaled = number * level * marks[3 + c, i].astype(jnp.float32)
            trace = scaled if trace is None else trace + scaled
        trace = trace.astype(jnp.bfloat16).astype(jnp.float32)
        turned = pltpu.roll(trace, 128 - shift, 1)
        following = pltpu.roll(turned, 39, 0)
        total[target] += jnp.where(lag < 128 - shift, turned[:32], following[:32])

    def several(step, carry):
        for u in range(UNROLL):
            one_pick(order[step * UNROLL + u])
        return carry

    whole = taken // UNROLL
    lax.fori_loop(0, whole, several, 0)

    def rest(step, carry):
        for u in range(4):
            one_pick(order[step * 4 + u])
        return carry

    lax.fori_loop(whole * (UNROLL // 4), (taken + 3) // 4, rest, 0)
    extra[...] = total[: extra.shape[0]].astype(extra.dtype)


def stack_kernel(parts, out, total):
    rows = out.shape[0]
    summed = parts[0].astype(jnp.float32)
    for p in range(1, parts.shape[0]):
        summed = summed + parts[p].astype(jnp.float32)
    cube = summed.reshape(rows, 32, 128)
    square = jnp.sum(jnp.sum(cube * cube, axis=2, keepdims=True), axis=1, keepdims=True)
    level = jnp.sqrt(square / (32 * 128) + EPS)
    total[...] = (cube / level).reshape(rows * 32, 128)
    for b in range(32):
        out[:, b * 128 : b * 128 + 128] = total[pl.ds(b, rows, stride=32), :]


def on_device(records, templates, pick_owner, pick_local, moveout, channel_mask):
    own_templates, pick_count, channels, taps = templates.shape
    columns = lax.axis_size("tpl")
    lines = lax.axis_size("sta")
    rows = own_templates * pick_count
    per_source = CAP * lines
    slots = columns * per_source
    anywhere = pl.BlockSpec(memory_space=pl.ANY)
    vmem, smem = pl.BlockSpec(memory_space=pltpu.VMEM), pl.BlockSpec(memory_space=pltpu.SMEM)

    here = lax.axis_index("sta").astype(jnp.int32).reshape(1)
    half = records.shape[0] // 2
    outbox, first, second = pl.pallas_call(
        functools.partial(front_kernel, per_source),
        out_shape=(
            jax.ShapeDtypeStruct((slots, channels * 256), jnp.bfloat16),
            jax.ShapeDtypeStruct((half, 112, 128), jnp.bfloat16),
            jax.ShapeDtypeStruct((half, 112, 128), jnp.bfloat16),
        ),
        in_specs=[smem] + [vmem] * 6,
        out_specs=(vmem, vmem, vmem),
        scratch_shapes=[pltpu.VMEM((records.shape[0] * 112, 128), jnp.float32)],
        compiler_params=pltpu.CompilerParams(vmem_limit_bytes=60 * 2**20),
    )(
        here,
        pick_owner.T,
        pick_local.T,
        moveout.T,
        channel_mask.transpose(1, 2, 0),
        templates.transpose(1, 2, 0, 3),
        records.transpose(1, 0, 2),
    )
    around = ring(first, second, "x")
    near_first = jnp.concatenate((first, second) + around[:2])
    near_second = jnp.concatenate(around[2:])
    inbox = lax.all_to_all(
        outbox.reshape(columns, per_source, channels * 256),
        "tpl",
        split_axis=0,
        concat_axis=0,
        tiled=True,
    )
    total_rows = columns * own_templates
    shapes, marks, power, near_first, near_second = pl.pallas_call(
        unpack_kernel,
        out_shape=(
            pltpu.VMEM((slots * 8 + 8, 128), jnp.float32),
            jax.ShapeDtypeStruct((16, slots + 128), jnp.int32),
            jax.ShapeDtypeStruct((8, slots + 128), jnp.float32),
            jax.ShapeDtypeStruct((4 * half, 112, 128), jnp.bfloat16),
            jax.ShapeDtypeStruct((4 * half, 112, 128), jnp.bfloat16),
        ),
        in_specs=[vmem, anywhere, anywhere],
        out_specs=(vmem, vmem, vmem, anywhere, anywhere),
        input_output_aliases={1: 3, 2: 4},
        compiler_params=pltpu.CompilerParams(vmem_limit_bytes=20 * 2**20),
    )(inbox.reshape(slots, channels * 256), near_first, near_second)
    shapes = pltpu.with_memory_space_constraint(shapes, pltpu.VMEM)

    def run_stage(stage, gathered, carried):
        scratch = [
            pltpu.VMEM((STATIONS[stage], 112, 128), jnp.bfloat16),
            pltpu.VMEM((STATIONS[stage] * 3, 48, 384), jnp.bfloat16),
            pltpu.VMEM((STATIONS[stage] * 3, 40, 128), jnp.float32),
            pltpu.VMEM((16 * 112, 128), jnp.float32),
            pltpu.VMEM((16 * 112, 256), jnp.float32),
            pltpu.SMEM((slots + 128,), jnp.int32),
            pltpu.SemaphoreType.DMA((PIECES[stage],)),
        ]
        result = pltpu.VMEM((total_rows, 32, 128), jnp.float32)
        extra = jax.ShapeDtypeStruct((total_rows if stage == 3 else 1, 32, 128), jnp.bfloat16)
        carried = [pltpu.with_memory_space_constraint(p, pltpu.VMEM) for p in carried]
        return pl.pallas_call(
            functools.partial(pick_kernel, stage, per_source, taps),
            out_shape=(result, extra),
            in_specs=[smem, smem, vmem] + [anywhere] * PIECES[stage] + [vmem] * len(carried),
            out_specs=(vmem, vmem),
            scratch_shapes=scratch,
            input_output_aliases={3 + PIECES[stage]: 0} if carried else {},
            cost_estimate=pl.CostEstimate(flops=0, bytes_accessed=30 * 10**6, transcendentals=0),
            compiler_params=pltpu.CompilerParams(vmem_limit_bytes=48 * 2**20),
        )(marks, power, shapes, *gathered, *carried)

    partial, token = run_stage(0, (near_first, near_second), ())

    def after(first, second):
        return pl.pallas_call(
            after_kernel,
            out_shape=tuple(jax.ShapeDtypeStruct(x.shape, x.dtype) for x in (first, second)),
            in_specs=[anywhere] * 3,
            out_specs=(anywhere, anywhere),
            input_output_aliases={0: 0, 1: 1},
            compiler_params=pltpu.CompilerParams(vmem_limit_bytes=2**20),
        )(first, second, token)

    far = ring(near_first, near_second, "z", after)
    partial, _ = run_stage(1, (far[0], far[3]), (partial,))
    partial, _ = run_stage(2, (far[1], far[2]), (partial,))
    _, partial = run_stage(3, (far[4], far[5]), (partial,))

    returned = lax.all_to_all(
        partial.reshape(columns, own_templates * 32, 128), "tpl", split_axis=0, concat_axis=0, tiled=True
    )
    return pl.pallas_call(
        stack_kernel,
        out_shape=jax.ShapeDtypeStruct((own_templates, 4096), jnp.float32),
        in_specs=[vmem],
        out_specs=vmem,
        scratch_shapes=[pltpu.VMEM((own_templates * 32, 128), jnp.float32)],
        compiler_params=pltpu.CompilerParams(vmem_limit_bytes=20 * 2**20),
    )(returned)


def solution(mesh):
    return jax.shard_map(
        on_device,
        mesh=mesh,
        in_specs=(
            P(("sta", "tpl"), None, None),
            P(("sta", "tpl"), None, None, None),
            P(("sta", "tpl"), None),
            P(("sta", "tpl"), None),
            P(("sta", "tpl"), None),
            P(("sta", "tpl"), None, None),
        ),
        out_specs=P(("sta", "tpl"), None),
        check_vma=False,
    )
```

```python
import functools

import jax
import jax.numpy as jnp
from jax import lax
from jax.experimental import pallas as pl
from jax.experimental.pallas import tpu as pltpu
from jax.sharding import PartitionSpec as P

EPS = 1e-06
CAP = 3
SIDE = 4
UNROLL = 16
INFO = 16
PIECES = (2, 2, 2, 2)
FIRST = (0, 32, 64, 96)
STATIONS = (32, 32, 32, 32)


def shifted(axis, step):
    if axis == "x":
        return [(x * SIDE + z, ((x + step) % SIDE) * SIDE + z) for x in range(SIDE) for z in range(SIDE)]
    return [(x * SIDE + z, x * SIDE + (z + step) % SIDE) for x in range(SIDE) for z in range(SIDE)]


def after_kernel(first, second, token, same_first, same_second):
    pass


def ring(first, second, axis, between=None):
    behind_first = lax.ppermute(first, "sta", shifted(axis, 1))
    ahead_second = lax.ppermute(second, "sta", shifted(axis, -1))
    behind_second = lax.ppermute(second, "sta", shifted(axis, 1))
    ahead_first = lax.ppermute(first, "sta", shifted(axis, -1))
    if between is not None:
        behind_first, ahead_second = between(behind_first, ahead_second)
    far_first = lax.ppermute(behind_first, "sta", shifted(axis, 1))
    far_second = lax.ppermute(ahead_second, "sta", shifted(axis, -1))
    return behind_first, behind_second, ahead_first, ahead_second, far_first, far_second


def front_kernel(per_source, here, owner, local, shift, mask, templates, records, outbox, first, second, spread):
    pick_count, channels, own_templates, taps = templates.shape
    rows = pick_count * own_templates
    for c in range(channels):
        for b in range(35):
            block = records[c, :, b * 128 : b * 128 + 128].astype(jnp.float32)
            spread[pl.ds(c * 35 + b, 8, stride=112), :] = block
    for b in range(105, 112):
        spread[pl.ds(b, 8, stride=112), :] = jnp.zeros((8, 128), jnp.float32)
    half = first.shape[0] * 112
    first[...] = spread[:half].reshape(first.shape).astype(first.dtype)
    second[...] = spread[half:].reshape(second.shape).astype(second.dtype)

    def flat(table):
        return jnp.concatenate([table[p : p + 1] for p in range(pick_count)], axis=1)

    owner, local, shift = flat(owner[...]), flat(local[...]), flat(shift[...])
    line, column = owner >> 3, owner & 7
    ahead_x = ((line >> 2) - (here[0] >> 2)) & 3
    ahead_z = ((line & 3) - (here[0] & 3)) & 3
    order_x = jnp.where(ahead_x == 3, 1, jnp.where(ahead_x == 0, 0, ahead_x + 1))
    order_z = jnp.where(ahead_z == 3, 1, jnp.where(ahead_z == 0, 0, ahead_z + 1))
    near = 8 * order_x + local
    early = jnp.where(near < 16, 1, 2) == order_z
    stage = jnp.where(order_z == 0, 0, jnp.where(early, 1, jnp.where(order_z == 3, 3, 2)))
    late = near + jnp.where(order_z == 1, 48, jnp.where(order_z == 2, 80, 96))
    station = jnp.where(stage == 0, near, jnp.where(early, 32 + near, late))
    bins = lax.broadcasted_iota(jnp.int32, (128, rows), 0)
    own = 4 * column + stage == bins
    hot = jnp.where(own, 1.0, 0.0)
    upper = lax.broadcasted_iota(jnp.int32, (rows, rows), 0) < lax.broadcasted_iota(jnp.int32, (rows, rows), 1)
    upper = jnp.where(upper, 1.0, 0.0).astype(jnp.bfloat16)
    before = jnp.dot(hot.astype(jnp.bfloat16), upper, preferred_element_type=jnp.float32)
    held = jnp.broadcast_to(jnp.sum(hot, axis=1, keepdims=True), (128, 128))
    i = lax.broadcasted_iota(jnp.int32, (128, 128), 0)
    j = lax.broadcasted_iota(jnp.int32, (128, 128), 1)
    earlier = jnp.where(((i >> 2) == (j >> 2)) & (j < i), 1.0, 0.0).astype(jnp.bfloat16)
    starts = jnp.dot(earlier, held.astype(jnp.bfloat16), preferred_element_type=jnp.float32)[:, 0:1]
    rank = jnp.sum(jnp.where(own, before + starts, 0.0), axis=0, keepdims=True).astype(jnp.int32)
    position = column * per_source + rank
    template = lax.broadcasted_iota(jnp.int32, (1, rows), 1)
    template = template - own_templates * ((template * 683) >> 14)
    facts = [station, shift, template] + [flat(mask[:, c, :]) for c in range(channels)]
    facts = [fact.astype(jnp.float32) for fact in facts] + [jnp.ones((1, rows), jnp.float32)]
    for k in range(4):
        facts.append(jnp.sum(jnp.where(bins == 4 * column + k, held[:, 0:1], 0.0), axis=0, keepdims=True))
    facts.append(jnp.zeros((16 - len(facts), rows), jnp.float32))
    facts = jnp.concatenate(facts, axis=0).astype(jnp.bfloat16)
    slot = lax.broadcasted_iota(jnp.int32, (outbox.shape[0], rows), 0)
    place = jnp.where(position == slot, 1.0, 0.0).astype(jnp.bfloat16)
    i = lax.broadcasted_iota(jnp.int32, (taps, 256), 0)
    j = lax.broadcasted_iota(jnp.int32, (taps, 256), 1)
    turn = jnp.where(i == 255 - j, 1.0, 0.0).astype(jnp.bfloat16)
    for c in range(channels):
        block = templates[:, c].reshape(rows, taps)
        sent = jnp.dot(block, turn, preferred_element_type=jnp.float32).astype(jnp.bfloat16)
        placed = jnp.dot(place, sent, preferred_element_type=jnp.float32)
        if c == 0:
            i = lax.broadcasted_iota(jnp.int32, (16, 256), 0)
            j = lax.broadcasted_iota(jnp.int32, (16, 256), 1)
            lead = jnp.where(i == j, 1.0, 0.0).astype(jnp.bfloat16)
            known = lax.dot_general(place, facts, (((1,), (1,)), ((), ())), preferred_element_type=jnp.float32)
            placed = placed + jnp.dot(known.astype(jnp.bfloat16), lead, preferred_element_type=jnp.float32)
        outbox[:, 256 * c : 256 * c + 256] = placed.astype(jnp.bfloat16)


def unpack_kernel(inbox, first, second, shapes, marks, power, same_first, same_second):
    slots = inbox.shape[0]
    lanes = lax.broadcasted_iota(jnp.int32, (slots, 128), 1)
    info = inbox[:, 0:128].astype(jnp.float32)
    zero = jnp.zeros((16, 128), jnp.int32)
    for k in range(slots // 128):
        turned = jnp.transpose(info[k * 128 : k * 128 + 128])[:16].astype(jnp.int32)
        marks[:, k * 128 : k * 128 + 128] = turned
    marks[:, slots : slots + 128] = zero
    shapes[pl.ds(8 * slots, 8), :] = jnp.zeros((8, 128), jnp.float32)
    square = jnp.zeros((slots, 128), jnp.float32)
    for k in range(inbox.shape[1] // 128):
        block = inbox[:, k * 128 : k * 128 + 128].astype(jnp.float32)
        if k == 0:
            block = jnp.where(lanes < INFO, 0.0, block)
        shapes[pl.ds(k, slots, stride=8), :] = block
        square = jnp.where(lanes == k // 2, square + jnp.sum(block * block, axis=1, keepdims=True), square)
    for k in range(slots // 128):
        power[:, k * 128 : k * 128 + 128] = jnp.transpose(square[k * 128 : k * 128 + 128])[:8]
    power[:, slots : slots + 128] = jnp.zeros((8, 128), jnp.float32)


def pick_kernel(stage, per_source, taps, here, marks, power, shapes, *refs):
    pieces = refs[: PIECES[stage]]
    refs = refs[PIECES[stage] :]
    if stage > 0:
        refs = refs[1:]
    total, extras = refs[0], refs[1:-7]
    records, frames, energy, wide, sums, order, sem = refs[-7:]
    copies = []
    base = 0
    for number, piece in enumerate(pieces):
        size = piece.shape[0]
        copies.append((base, size, pltpu.make_async_copy(piece, records.at[pl.ds(base, size)], sem.at[number])))
        base += size
    for _, _, copy in copies:
        copy.start()
    if stage == 0:
        total[...] = jnp.zeros_like(total)

    taken = jnp.int32(0)
    for source in range(total.shape[0] // 24):
        first = jnp.int32(source * per_source)
        for earlier in range(stage):
            first = first + marks[7 + earlier, source * per_source]
        count = marks[7 + stage, source * per_source]

        def note(k, carry, first=first, taken=taken):
            order[taken + k] = first + k
            return carry

        lax.fori_loop(0, count, note, 0)
        taken = taken + count
    for u in range(UNROLL):
        order[taken + u] = jnp.int32(marks.shape[1] - 128)

    row = lax.broadcasted_iota(jnp.int32, (256, 256), 0) % 128
    column = lax.broadcasted_iota(jnp.int32, (256, 256), 1) % 128
    tail = taps - 128
    suffix = row >= column
    prefix = ((column < 128 - tail) & (row - column < tail)) | (column - row > 128 - tail)
    left = lax.broadcasted_iota(jnp.int32, (256, 256), 1) < 128
    band = jnp.where((left & suffix) | (~left & prefix), 1.0, 0.0).astype(jnp.bfloat16)
    near_side = lax.broadcasted_iota(jnp.int32, (40, 128), 1) < 128 - tail
    group = sums.shape[0] // 112

    def prepare(step, carry):
        x = records[pl.ds(step * group, group)].reshape(group * 112, 128).astype(jnp.float32)
        wide[...] = x
        square = x * x
        high = square.astype(jnp.bfloat16)
        low = (square - high.astype(jnp.float32)).astype(jnp.bfloat16)
        sums[...] = jnp.dot(jnp.concatenate([high, low], axis=1), band, preferred_element_type=jnp.float32)
        for s in range(group):
            for c in range(3):
                at = s * 112 + c * 35
                slot = (step * group + s) * 3 + c
                whole = jnp.broadcast_to(sums[at + 1 : at + 41, 0:128][:, 0:1], (40, 128))
                ending = jnp.where(
                    near_side, sums[at + 1 : at + 41, 128:256], whole + sums[at + 2 : at + 42, 128:256]
                )
                energy[slot] = sums[at : at + 40, 0:128] + ending
                for q in range(3):
                    frames[slot, 0:40, q * 128 : q * 128 + 128] = wide[at + q : at + q + 40, :].astype(jnp.bfloat16)
        return carry

    for first, size, copy in copies:
        copy.wait()
        lax.fori_loop(first // group, (first + size) // group, prepare, 0)

    across = lax.broadcasted_iota(jnp.int32, (128, 128), 1)
    below = across <= lax.broadcasted_iota(jnp.int32, (128, 128), 0)
    nothing = jnp.zeros((128, 128), jnp.bfloat16)
    lag = lax.broadcasted_iota(jnp.int32, (32, 128), 1)

    def spread(line):
        block = jnp.broadcast_to(line, (128, 128))
        return pltpu.roll(block, 1, 1, stride=1, stride_axis=0).astype(jnp.bfloat16)

    def one_pick(i):
        station = 3 * jnp.maximum(marks[0, i] - FIRST[stage], 0)
        shift = marks[1, i]
        target = marks[2, i] + 24 * jnp.minimum(i // per_source, 7)
        trace = None
        lines = shapes[pl.ds(pl.multiple_of(8 * i, 8), 8), :]
        for c in range(3):
            late = spread(lines[2 * c : 2 * c + 1])
            early = spread(lines[2 * c + 1 : 2 * c + 2])
            toeplitz = jnp.concatenate(
                [jnp.where(below, early, nothing), jnp.where(below, late, early), jnp.where(below, nothing, late)],
                axis=0,
            )
            number = jnp.dot(frames[station + c], toeplitz, preferred_element_type=jnp.float32)[:40]
            level = lax.rsqrt(power[c, i] * energy[station + c] + EPS)
            scaled = number * level * marks[3 + c, i].astype(jnp.float32)
            trace = scaled if trace is None else trace + scaled
        trace = trace.astype(jnp.bfloat16).astype(jnp.float32)
        turned = pltpu.roll(trace, 128 - shift, 1)
        following = pltpu.roll(turned, 39, 0)
        total[target] += jnp.where(lag < 128 - shift, turned[:32], following[:32])

    def several(step, carry):
        for u in range(UNROLL):
            one_pick(order[step * UNROLL + u])
        return carry

    whole = taken // UNROLL
    lax.fori_loop(0, whole, several, 0)

    def rest(step, carry):
        for u in range(4):
            one_pick(order[step * 4 + u])
        return carry

    lax.fori_loop(whole * (UNROLL // 4), (taken + 3) // 4, rest, 0)
    for step, extra in enumerate(extras):
        rows = extra.shape[0]
        target = (here[0] + step) & 7 if stage == len(PIECES) - 1 else 0
        extra[...] = total[pl.ds(target * rows, rows)].astype(extra.dtype)


def stack_kernel(*refs):
    parts, (out, total) = refs[:-2], refs[-2:]
    rows = out.shape[0]
    cube = parts[0][...].astype(jnp.float32)
    for part in parts[1:]:
        cube = cube + part[...].astype(jnp.float32)
    square = jnp.sum(jnp.sum(cube * cube, axis=2, keepdims=True), axis=1, keepdims=True)
    level = jnp.sqrt(square / (32 * 128) + EPS)
    total[...] = (cube / level).reshape(rows * 32, 128)
    for b in range(32):
        out[:, b * 128 : b * 128 + 128] = total[pl.ds(b, rows, stride=32), :]


def on_device(records, templates, pick_owner, pick_local, moveout, channel_mask):
    own_templates, pick_count, channels, taps = templates.shape
    columns = lax.axis_size("tpl")
    lines = lax.axis_size("sta")
    rows = own_templates * pick_count
    per_source = CAP * lines
    slots = columns * per_source
    anywhere = pl.BlockSpec(memory_space=pl.ANY)
    vmem, smem = pl.BlockSpec(memory_space=pltpu.VMEM), pl.BlockSpec(memory_space=pltpu.SMEM)

    here = lax.axis_index("sta").astype(jnp.int32).reshape(1)
    half = records.shape[0] // 2
    outbox, first, second = pl.pallas_call(
        functools.partial(front_kernel, per_source),
        out_shape=(
            jax.ShapeDtypeStruct((slots, channels * 256), jnp.bfloat16),
            jax.ShapeDtypeStruct((half, 112, 128), jnp.bfloat16),
            jax.ShapeDtypeStruct((half, 112, 128), jnp.bfloat16),
        ),
        in_specs=[smem] + [vmem] * 6,
        out_specs=(vmem, vmem, vmem),
        scratch_shapes=[pltpu.VMEM((records.shape[0] * 112, 128), jnp.float32)],
        compiler_params=pltpu.CompilerParams(vmem_limit_bytes=60 * 2**20),
    )(
        here,
        pick_owner.T,
        pick_local.T,
        moveout.T,
        channel_mask.transpose(1, 2, 0),
        templates.transpose(1, 2, 0, 3),
        records.transpose(1, 0, 2),
    )
    around = ring(first, second, "x")
    near_first = jnp.concatenate((first, second) + around[:2])
    near_second = jnp.concatenate(around[2:])
    inbox = lax.all_to_all(
        outbox.reshape(columns, per_source, channels * 256),
        "tpl",
        split_axis=0,
        concat_axis=0,
        tiled=True,
    )
    total_rows = columns * own_templates
    shapes, marks, power, near_first, near_second = pl.pallas_call(
        unpack_kernel,
        out_shape=(
            pltpu.VMEM((slots * 8 + 8, 128), jnp.float32),
            jax.ShapeDtypeStruct((16, slots + 128), jnp.int32),
            jax.ShapeDtypeStruct((8, slots + 128), jnp.float32),
            jax.ShapeDtypeStruct((4 * half, 112, 128), jnp.bfloat16),
            jax.ShapeDtypeStruct((4 * half, 112, 128), jnp.bfloat16),
        ),
        in_specs=[vmem, anywhere, anywhere],
        out_specs=(vmem, vmem, vmem, anywhere, anywhere),
        input_output_aliases={1: 3, 2: 4},
        compiler_params=pltpu.CompilerParams(vmem_limit_bytes=20 * 2**20),
    )(inbox.reshape(slots, channels * 256), near_first, near_second)
    shapes = pltpu.with_memory_space_constraint(shapes, pltpu.VMEM)

    place = lax.axis_index("tpl").astype(jnp.int32).reshape(1)

    def run_stage(stage, gathered, carried):
        scratch = [
            pltpu.VMEM((STATIONS[stage], 112, 128), jnp.bfloat16),
            pltpu.VMEM((STATIONS[stage] * 3, 48, 384), jnp.bfloat16),
            pltpu.VMEM((STATIONS[stage] * 3, 40, 128), jnp.float32),
            pltpu.VMEM((16 * 112, 128), jnp.float32),
            pltpu.VMEM((16 * 112, 256), jnp.float32),
            pltpu.SMEM((slots + 128,), jnp.int32),
            pltpu.SemaphoreType.DMA((PIECES[stage],)),
        ]
        result = pltpu.VMEM((total_rows, 32, 128), jnp.float32)
        if stage == len(PIECES) - 1:
            extras = (jax.ShapeDtypeStruct((own_templates, 32, 128), jnp.bfloat16),) * columns
        else:
            extras = (jax.ShapeDtypeStruct((1, 32, 128), jnp.bfloat16),)
        carried = [pltpu.with_memory_space_constraint(p, pltpu.VMEM) for p in carried]
        return pl.pallas_call(
            functools.partial(pick_kernel, stage, per_source, taps),
            out_shape=(result,) + extras,
            in_specs=[smem, smem, smem, vmem] + [anywhere] * PIECES[stage] + [vmem] * len(carried),
            out_specs=(vmem,) * (1 + len(extras)),
            scratch_shapes=scratch,
            input_output_aliases={4 + PIECES[stage]: 0} if carried else {},
            cost_estimate=pl.CostEstimate(flops=0, bytes_accessed=30 * 10**6, transcendentals=0),
            compiler_params=pltpu.CompilerParams(vmem_limit_bytes=48 * 2**20),
        )(place, marks, power, shapes, *gathered, *carried)

    partial, token = run_stage(0, (near_first, near_second), ())

    def after(first, second):
        return pl.pallas_call(
            after_kernel,
            out_shape=tuple(jax.ShapeDtypeStruct(x.shape, x.dtype) for x in (first, second)),
            in_specs=[anywhere] * 3,
            out_specs=(anywhere, anywhere),
            input_output_aliases={0: 0, 1: 1},
            compiler_params=pltpu.CompilerParams(vmem_limit_bytes=2**20),
        )(first, second, token)

    far = ring(near_first, near_second, "z", after)
    partial, _ = run_stage(1, (far[0], far[3]), (partial,))
    partial, _ = run_stage(2, (far[1], far[2]), (partial,))
    _, *partial = run_stage(3, (far[4], far[5]), (partial,))

    returned = [
        lax.ppermute(part, "tpl", [(i, (i + step) % columns) for i in range(columns)]) if step else part
        for step, part in enumerate(partial)
    ]
    return pl.pallas_call(
        stack_kernel,
        out_shape=jax.ShapeDtypeStruct((own_templates, 4096), jnp.float32),
        in_specs=[vmem] * columns,
        out_specs=vmem,
        scratch_shapes=[pltpu.VMEM((own_templates * 32, 128), jnp.float32)],
        compiler_params=pltpu.CompilerParams(vmem_limit_bytes=20 * 2**20),
    )(*returned)


def solution(mesh):
    return jax.shard_map(
        on_device,
        mesh=mesh,
        in_specs=(
            P(("sta", "tpl"), None, None),
            P(("sta", "tpl"), None, None, None),
            P(("sta", "tpl"), None),
            P(("sta", "tpl"), None),
            P(("sta", "tpl"), None),
            P(("sta", "tpl"), None, None),
        ),
        out_specs=P(("sta", "tpl"), None),
        check_vma=False,
    )
```

```python
import functools

import jax
import jax.numpy as jnp
from jax import lax
from jax.experimental import pallas as pl
from jax.experimental.pallas import tpu as pltpu
from jax.sharding import PartitionSpec as P

EPS = 1e-06
CAP = 3
SIDE = 4
UNROLL = 16
INFO = 16
PIECES = (2, 2, 2, 2)
FIRST = (0, 32, 64, 96)
STATIONS = (32, 32, 32, 32)


def shifted(axis, step):
    if axis == "x":
        return [(x * SIDE + z, ((x + step) % SIDE) * SIDE + z) for x in range(SIDE) for z in range(SIDE)]
    return [(x * SIDE + z, x * SIDE + (z + step) % SIDE) for x in range(SIDE) for z in range(SIDE)]


def after_kernel(first, second, token, same_first, same_second):
    pass


def ring(first, second, axis, between=None):
    behind_first = lax.ppermute(first, "sta", shifted(axis, 1))
    ahead_second = lax.ppermute(second, "sta", shifted(axis, -1))
    behind_second = lax.ppermute(second, "sta", shifted(axis, 1))
    ahead_first = lax.ppermute(first, "sta", shifted(axis, -1))
    if between is not None:
        behind_first, ahead_second = between(behind_first, ahead_second)
    far_first = lax.ppermute(behind_first, "sta", shifted(axis, 1))
    far_second = lax.ppermute(ahead_second, "sta", shifted(axis, -1))
    return behind_first, behind_second, ahead_first, ahead_second, far_first, far_second


def front_kernel(per_source, here, owner, local, shift, mask, templates, records, outbox, first, second, spread):
    pick_count, channels, own_templates, taps = templates.shape
    rows = pick_count * own_templates
    for c in range(channels):
        for b in range(35):
            block = records[c, :, b * 128 : b * 128 + 128].astype(jnp.float32)
            spread[pl.ds(c * 35 + b, 8, stride=112), :] = block
    for b in range(105, 112):
        spread[pl.ds(b, 8, stride=112), :] = jnp.zeros((8, 128), jnp.float32)
    half = first.shape[0] * 112
    first[...] = spread[:half].reshape(first.shape).astype(first.dtype)
    second[...] = spread[half:].reshape(second.shape).astype(second.dtype)

    def flat(table):
        return jnp.concatenate([table[p : p + 1] for p in range(pick_count)], axis=1)

    owner, local, shift = flat(owner[...]), flat(local[...]), flat(shift[...])
    line, column = owner >> 3, owner & 7
    ahead_x = ((line >> 2) - (here[0] >> 2)) & 3
    ahead_z = ((line & 3) - (here[0] & 3)) & 3
    order_x = jnp.where(ahead_x == 3, 1, jnp.where(ahead_x == 0, 0, ahead_x + 1))
    order_z = jnp.where(ahead_z == 3, 1, jnp.where(ahead_z == 0, 0, ahead_z + 1))
    near = 8 * order_x + local
    early = jnp.where(near < 16, 1, 2) == order_z
    stage = jnp.where(order_z == 0, 0, jnp.where(early, 1, jnp.where(order_z == 3, 3, 2)))
    late = near + jnp.where(order_z == 1, 48, jnp.where(order_z == 2, 80, 96))
    station = jnp.where(stage == 0, near, jnp.where(early, 32 + near, late))
    bins = lax.broadcasted_iota(jnp.int32, (128, rows), 0)
    own = 4 * column + stage == bins
    hot = jnp.where(own, 1.0, 0.0)
    upper = lax.broadcasted_iota(jnp.int32, (rows, rows), 0) < lax.broadcasted_iota(jnp.int32, (rows, rows), 1)
    upper = jnp.where(upper, 1.0, 0.0).astype(jnp.bfloat16)
    before = jnp.dot(hot.astype(jnp.bfloat16), upper, preferred_element_type=jnp.float32)
    held = jnp.broadcast_to(jnp.sum(hot, axis=1, keepdims=True), (128, 128))
    i = lax.broadcasted_iota(jnp.int32, (128, 128), 0)
    j = lax.broadcasted_iota(jnp.int32, (128, 128), 1)
    earlier = jnp.where(((i >> 2) == (j >> 2)) & (j < i), 1.0, 0.0).astype(jnp.bfloat16)
    starts = jnp.dot(earlier, held.astype(jnp.bfloat16), preferred_element_type=jnp.float32)[:, 0:1]
    rank = jnp.sum(jnp.where(own, before + starts, 0.0), axis=0, keepdims=True).astype(jnp.int32)
    position = column * per_source + rank
    template = lax.broadcasted_iota(jnp.int32, (1, rows), 1)
    template = template - own_templates * ((template * 683) >> 14)
    facts = [station, shift, template] + [flat(mask[:, c, :]) for c in range(channels)]
    facts = [fact.astype(jnp.float32) for fact in facts] + [jnp.ones((1, rows), jnp.float32)]
    for k in range(4):
        facts.append(jnp.sum(jnp.where(bins == 4 * column + k, held[:, 0:1], 0.0), axis=0, keepdims=True))
    facts.append(jnp.zeros((16 - len(facts), rows), jnp.float32))
    facts = jnp.concatenate(facts, axis=0).astype(jnp.bfloat16)
    slot = lax.broadcasted_iota(jnp.int32, (outbox.shape[0], rows), 0)
    place = jnp.where(position == slot, 1.0, 0.0).astype(jnp.bfloat16)
    i = lax.broadcasted_iota(jnp.int32, (taps, 256), 0)
    j = lax.broadcasted_iota(jnp.int32, (taps, 256), 1)
    turn = jnp.where(i == 255 - j, 1.0, 0.0).astype(jnp.bfloat16)
    for c in range(channels):
        block = templates[:, c].reshape(rows, taps)
        sent = jnp.dot(block, turn, preferred_element_type=jnp.float32).astype(jnp.bfloat16)
        placed = jnp.dot(place, sent, preferred_element_type=jnp.float32)
        if c == 0:
            i = lax.broadcasted_iota(jnp.int32, (16, 256), 0)
            j = lax.broadcasted_iota(jnp.int32, (16, 256), 1)
            lead = jnp.where(i == j, 1.0, 0.0).astype(jnp.bfloat16)
            known = lax.dot_general(place, facts, (((1,), (1,)), ((), ())), preferred_element_type=jnp.float32)
            placed = placed + jnp.dot(known.astype(jnp.bfloat16), lead, preferred_element_type=jnp.float32)
        outbox[:, 256 * c : 256 * c + 256] = placed.astype(jnp.bfloat16)


def unpack_kernel(inbox, first, second, shapes, marks, power, same_first, same_second):
    slots = inbox.shape[0]
    lanes = lax.broadcasted_iota(jnp.int32, (slots, 128), 1)
    info = inbox[:, 0:128].astype(jnp.float32)
    zero = jnp.zeros((16, 128), jnp.int32)
    for k in range(slots // 128):
        turned = jnp.transpose(info[k * 128 : k * 128 + 128])[:16].astype(jnp.int32)
        marks[:, k * 128 : k * 128 + 128] = turned
    marks[:, slots : slots + 128] = zero
    shapes[pl.ds(8 * slots, 8), :] = jnp.zeros((8, 128), jnp.float32)
    square = jnp.zeros((slots, 128), jnp.float32)
    for k in range(inbox.shape[1] // 128):
        block = inbox[:, k * 128 : k * 128 + 128].astype(jnp.float32)
        if k == 0:
            block = jnp.where(lanes < INFO, 0.0, block)
        shapes[pl.ds(k, slots, stride=8), :] = block
        square = jnp.where(lanes == k // 2, square + jnp.sum(block * block, axis=1, keepdims=True), square)
    for k in range(slots // 128):
        power[:, k * 128 : k * 128 + 128] = jnp.transpose(square[k * 128 : k * 128 + 128])[:8]
    power[:, slots : slots + 128] = jnp.zeros((8, 128), jnp.float32)


def pick_kernel(stage, per_source, taps, here, marks, power, shapes, *refs):
    pieces = refs[: PIECES[stage]]
    refs = refs[PIECES[stage] :]
    if stage > 0:
        refs = refs[1:]
    total, extras = refs[0], refs[1:-7]
    records, frames, energy, wide, sums, order, sem = refs[-7:]
    copies = []
    base = 0
    for number, piece in enumerate(pieces):
        size = piece.shape[0]
        copies.append((base, size, pltpu.make_async_copy(piece, records.at[pl.ds(base, size)], sem.at[number])))
        base += size
    for _, _, copy in copies:
        copy.start()
    if stage == 0:
        total[...] = jnp.zeros_like(total)

    taken = jnp.int32(0)
    for source in range(total.shape[0] // 24):
        first = jnp.int32(source * per_source)
        for earlier in range(stage):
            first = first + marks[7 + earlier, source * per_source]
        count = marks[7 + stage, source * per_source]

        def note(k, carry, first=first, taken=taken):
            order[taken + k] = first + k
            return carry

        lax.fori_loop(0, count, note, 0)
        taken = taken + count
    for u in range(UNROLL):
        order[taken + u] = jnp.int32(marks.shape[1] - 128)

    row = lax.broadcasted_iota(jnp.int32, (256, 256), 0) % 128
    column = lax.broadcasted_iota(jnp.int32, (256, 256), 1) % 128
    tail = taps - 128
    suffix = row >= column
    prefix = ((column < 128 - tail) & (row - column < tail)) | (column - row > 128 - tail)
    left = lax.broadcasted_iota(jnp.int32, (256, 256), 1) < 128
    band = jnp.where((left & suffix) | (~left & prefix), 1.0, 0.0).astype(jnp.bfloat16)
    near_side = lax.broadcasted_iota(jnp.int32, (40, 128), 1) < 128 - tail
    group = sums.shape[0] // 112

    def prepare(step, carry):
        x = records[pl.ds(step * group, group)].reshape(group * 112, 128).astype(jnp.float32)
        wide[...] = x
        square = x * x
        high = square.astype(jnp.bfloat16)
        low = (square - high.astype(jnp.float32)).astype(jnp.bfloat16)
        sums[...] = jnp.dot(jnp.concatenate([high, low], axis=1), band, preferred_element_type=jnp.float32)
        for s in range(group):
            for c in range(3):
                at = s * 112 + c * 35
                slot = (step * group + s) * 3 + c
                whole = jnp.broadcast_to(sums[at + 1 : at + 41, 0:128][:, 0:1], (40, 128))
                ending = jnp.where(
                    near_side, sums[at + 1 : at + 41, 128:256], whole + sums[at + 2 : at + 42, 128:256]
                )
                energy[slot] = sums[at : at + 40, 0:128] + ending
                for q in range(3):
                    frames[slot, 0:40, q * 128 : q * 128 + 128] = wide[at + q : at + q + 40, :].astype(jnp.bfloat16)
        return carry

    for first, size, copy in copies:
        copy.wait()
        lax.fori_loop(first // group, (first + size) // group, prepare, 0)

    across = lax.broadcasted_iota(jnp.int32, (128, 128), 1)
    below = across <= lax.broadcasted_iota(jnp.int32, (128, 128), 0)
    nothing = jnp.zeros((128, 128), jnp.bfloat16)
    lag = lax.broadcasted_iota(jnp.int32, (32, 128), 1)

    def spread(line):
        block = jnp.broadcast_to(line, (128, 128))
        return pltpu.roll(block, 1, 1, stride=1, stride_axis=0).astype(jnp.bfloat16)

    def one_pick(i):
        station = 3 * jnp.maximum(marks[0, i] - FIRST[stage], 0)
        shift = marks[1, i]
        target = marks[2, i] + 24 * jnp.minimum(i // per_source, 7)
        trace = None
        lines = shapes[pl.ds(pl.multiple_of(8 * i, 8), 8), :]
        for c in range(3):
            late = spread(lines[2 * c : 2 * c + 1])
            early = spread(lines[2 * c + 1 : 2 * c + 2])
            toeplitz = jnp.concatenate(
                [jnp.where(below, early, nothing), jnp.where(below, late, early), jnp.where(below, nothing, late)],
                axis=0,
            )
            number = jnp.dot(frames[station + c], toeplitz, preferred_element_type=jnp.float32)[:40]
            level = lax.rsqrt(power[c, i] * energy[station + c] + EPS)
            scaled = number * level * marks[3 + c, i].astype(jnp.float32)
            trace = scaled if trace is None else trace + scaled
        trace = trace.astype(jnp.bfloat16).astype(jnp.float32)
        turned = pltpu.roll(trace, 128 - shift, 1)
        following = pltpu.roll(turned, 39, 0)
        total[target] += jnp.where(lag < 128 - shift, turned[:32], following[:32])

    def several(step, carry):
        for u in range(UNROLL):
            one_pick(order[step * UNROLL + u])
        return carry

    whole = taken // UNROLL
    lax.fori_loop(0, whole, several, 0)

    def rest(step, carry):
        for u in range(4):
            one_pick(order[step * 4 + u])
        return carry

    lax.fori_loop(whole * (UNROLL // 4), (taken + 3) // 4, rest, 0)
    for step, extra in enumerate(extras):
        rows = extra.shape[0]
        target = (here[0] + step) & 7 if stage == len(PIECES) - 1 else 0
        extra[...] = total[pl.ds(target * rows, rows)].astype(extra.dtype)


def stack_kernel(*refs):
    parts, (out, total) = refs[:-2], refs[-2:]
    rows = out.shape[0]
    cube = parts[0][...].astype(jnp.float32)
    for part in parts[1:]:
        cube = cube + part[...].astype(jnp.float32)
    square = jnp.sum(jnp.sum(cube * cube, axis=2, keepdims=True), axis=1, keepdims=True)
    level = jnp.sqrt(square / (32 * 128) + EPS)
    total[...] = (cube / level).reshape(rows * 32, 128)
    for b in range(32):
        out[:, b * 128 : b * 128 + 128] = total[pl.ds(b, rows, stride=32), :]


def on_device(records, templates, pick_owner, pick_local, moveout, channel_mask):
    own_templates, pick_count, channels, taps = templates.shape
    columns = lax.axis_size("tpl")
    lines = lax.axis_size("sta")
    rows = own_templates * pick_count
    per_source = CAP * lines
    slots = columns * per_source
    anywhere = pl.BlockSpec(memory_space=pl.ANY)
    vmem, smem = pl.BlockSpec(memory_space=pltpu.VMEM), pl.BlockSpec(memory_space=pltpu.SMEM)

    here = lax.axis_index("sta").astype(jnp.int32).reshape(1)
    half = records.shape[0] // 2
    outbox, first, second = pl.pallas_call(
        functools.partial(front_kernel, per_source),
        out_shape=(
            jax.ShapeDtypeStruct((slots, channels * 256), jnp.bfloat16),
            jax.ShapeDtypeStruct((half, 112, 128), jnp.bfloat16),
            jax.ShapeDtypeStruct((half, 112, 128), jnp.bfloat16),
        ),
        in_specs=[smem] + [vmem] * 6,
        out_specs=(vmem, vmem, vmem),
        scratch_shapes=[pltpu.VMEM((records.shape[0] * 112, 128), jnp.float32)],
        compiler_params=pltpu.CompilerParams(vmem_limit_bytes=60 * 2**20),
    )(
        here,
        pick_owner.T,
        pick_local.T,
        moveout.T,
        channel_mask.transpose(1, 2, 0),
        templates.transpose(1, 2, 0, 3),
        records.transpose(1, 0, 2),
    )
    around = ring(first, second, "x")
    near_first = jnp.concatenate((first, second) + around[:2])
    near_second = jnp.concatenate(around[2:])
    inbox = lax.all_to_all(
        outbox.reshape(columns, per_source, channels * 256),
        "tpl",
        split_axis=0,
        concat_axis=0,
        tiled=True,
    )
    total_rows = columns * own_templates
    shapes, marks, power, near_first, near_second = pl.pallas_call(
        unpack_kernel,
        out_shape=(
            pltpu.VMEM((slots * 8 + 8, 128), jnp.float32),
            jax.ShapeDtypeStruct((16, slots + 128), jnp.int32),
            jax.ShapeDtypeStruct((8, slots + 128), jnp.float32),
            jax.ShapeDtypeStruct((4 * half, 112, 128), jnp.bfloat16),
            jax.ShapeDtypeStruct((4 * half, 112, 128), jnp.bfloat16),
        ),
        in_specs=[vmem, anywhere, anywhere],
        out_specs=(vmem, vmem, vmem, anywhere, anywhere),
        input_output_aliases={1: 3, 2: 4},
        compiler_params=pltpu.CompilerParams(vmem_limit_bytes=20 * 2**20),
    )(inbox.reshape(slots, channels * 256), near_first, near_second)
    shapes = pltpu.with_memory_space_constraint(shapes, pltpu.VMEM)

    place = lax.axis_index("tpl").astype(jnp.int32).reshape(1)

    def run_stage(stage, gathered, carried):
        scratch = [
            pltpu.VMEM((STATIONS[stage], 112, 128), jnp.bfloat16),
            pltpu.VMEM((STATIONS[stage] * 3, 48, 384), jnp.bfloat16),
            pltpu.VMEM((STATIONS[stage] * 3, 40, 128), jnp.float32),
            pltpu.VMEM((16 * 112, 128), jnp.float32),
            pltpu.VMEM((16 * 112, 256), jnp.float32),
            pltpu.SMEM((slots + 128,), jnp.int32),
            pltpu.SemaphoreType.DMA((PIECES[stage],)),
        ]
        result = pltpu.VMEM((total_rows, 32, 128), jnp.float32)
        if stage == len(PIECES) - 1:
            extras = (jax.ShapeDtypeStruct((own_templates, 32, 128), jnp.bfloat16),) * columns
        else:
            extras = (jax.ShapeDtypeStruct((1, 32, 128), jnp.bfloat16),)
        carried = [pltpu.with_memory_space_constraint(p, pltpu.VMEM) for p in carried]
        return pl.pallas_call(
            functools.partial(pick_kernel, stage, per_source, taps),
            out_shape=(result,) + extras,
            in_specs=[smem, smem, smem, vmem] + [anywhere] * PIECES[stage] + [vmem] * len(carried),
            out_specs=(vmem,) * (1 + len(extras)),
            scratch_shapes=scratch,
            input_output_aliases={4 + PIECES[stage]: 0} if carried else {},
            cost_estimate=pl.CostEstimate(flops=0, bytes_accessed=30 * 10**6, transcendentals=0),
            compiler_params=pltpu.CompilerParams(vmem_limit_bytes=24 * 2**20),
        )(place, marks, power, shapes, *gathered, *carried)

    partial, token = run_stage(0, (near_first, near_second), ())

    def after(first, second):
        return pl.pallas_call(
            after_kernel,
            out_shape=tuple(jax.ShapeDtypeStruct(x.shape, x.dtype) for x in (first, second)),
            in_specs=[anywhere] * 3,
            out_specs=(anywhere, anywhere),
            input_output_aliases={0: 0, 1: 1},
            compiler_params=pltpu.CompilerParams(vmem_limit_bytes=2**20),
        )(first, second, token)

    far = ring(near_first, near_second, "z", after)
    partial, _ = run_stage(1, (far[0], far[3]), (partial,))
    partial, _ = run_stage(2, (far[1], far[2]), (partial,))
    _, *partial = run_stage(3, (far[4], far[5]), (partial,))

    returned = [
        lax.ppermute(part, "tpl", [(i, (i + step) % columns) for i in range(columns)]) if step else part
        for step, part in enumerate(partial)
    ]
    return pl.pallas_call(
        stack_kernel,
        out_shape=jax.ShapeDtypeStruct((own_templates, 4096), jnp.float32),
        in_specs=[vmem] * columns,
        out_specs=vmem,
        scratch_shapes=[pltpu.VMEM((own_templates * 32, 128), jnp.float32)],
        compiler_params=pltpu.CompilerParams(vmem_limit_bytes=20 * 2**20),
    )(*returned)


def solution(mesh):
    return jax.shard_map(
        on_device,
        mesh=mesh,
        in_specs=(
            P(("sta", "tpl"), None, None),
            P(("sta", "tpl"), None, None, None),
            P(("sta", "tpl"), None),
            P(("sta", "tpl"), None),
            P(("sta", "tpl"), None),
            P(("sta", "tpl"), None, None),
        ),
        out_specs=P(("sta", "tpl"), None),
        check_vma=False,
    )
```
